32 devices in a mesh: state: 8 (over z, x), rank: 4 (over y, core).
Axes of the slice: x: 2, y: 2, z: 4, core: 2. Of those that a mesh axis runs over, the one named last changes fastest.
Arguments:
- token_ids: int32 [3, 128], replicated, may hold values from 0 to 9999
- word_emb: bfloat16 [10000, 128], replicated, may hold values from -6 to 6
- state_emb: bfloat16 [32768, 128], P('state'), may hold values from -3 to 3
- log_norm: float32 [32768], P('state'), may hold values from -0.5 to 1
- beta_last: bfloat16 [32768, 128], P('state'), may hold values from 0.19921875 to 5
- forward_marg: bfloat16 [32768, 384], P('state'), may hold values from 0.049804688 to 2
- trans_left: bfloat16 [32768, 2048], P('state', 'rank'), as said below
- trans_right: bfloat16 [32768, 2048], P('state', 'rank'), as said below
Outputs:
- beta_first: bfloat16 [32768, 128], P('state')
- grad_left: bfloat16 [32768, 2048], P('state', 'rank')
- grad_right: bfloat16 [32768, 2048], P('state', 'rank')
The draws below stay inside these ranges and needn't reach their ends.
Inputs may be any that keep to these rules, and one draw needn't show every extreme that they name: `trans_left`: positive entries. `trans_right`: positive entries.
All inputs are finite; a program needn't handle non-finite values.
Results may differ from the reference program's by a relative error of at most 0.009.
Values may be sent and summed in bfloat16 or wider, within the bound.
No kernel may reach another device: no remote copies, remote signals or barrier semaphores. Data moves between devices by JAX's collectives and lax.ppermute only.
A program may use at most 128 MiB of HBM per device.

```python
import math
import jax
import jax.numpy as jnp
import numpy as np
from jax import lax

R = 2048
H = 128
VOCAB = 10000
B = 128
STEPS = 3
S = 32768


def cluster_ids(key):
    groups = max(S // 512, 8)
    labels = jax.random.randint(jax.random.fold_in(key, 5), (S,), 0, groups)
    return (labels, groups)


def column_factor(key, labels, groups):
    table = jax.random.normal(key, (groups, R), jnp.float32)
    return jnp.exp(2.0 * jnp.take(table, labels, axis=0) - 2.0)


def draw_state_emb(key, part):
    labels, groups = cluster_ids(key)
    key = jax.random.fold_in(key, 37)
    first, second = jax.random.split(key)
    centers = jnp.clip(jax.random.normal(second, (groups, H), jnp.float32), -4.0, 4.0)
    noise = jnp.clip(jax.random.normal(first, (S, H), jnp.float32), -4.0, 4.0)
    values = (1.5 * jnp.take(centers, labels, axis=0) + noise) / math.sqrt(H)
    return values.astype(jnp.bfloat16)


def draw_trans_left(key, part):
    labels, groups = cluster_ids(key)
    key = jax.random.fold_in(key, 11)
    first = jax.random.fold_in(key, 0)
    third = jax.random.fold_in(key, 2)
    noise = jax.random.normal(first, (S, R), jnp.float32)
    rising = 1.0 + 2.0 * jnp.arange(S, dtype=jnp.float32)[:, None] / S
    factor = column_factor(third, labels, groups)
    return (jnp.exp(2.0 * noise - 2.0) * factor * rising).astype(jnp.bfloat16)


def draw_trans_right(key, part):
    labels, groups = cluster_ids(key)
    key = jax.random.fold_in(key, 23)
    first = jax.random.fold_in(key, 0)
    third = jax.random.fold_in(key, 2)
    noise = jax.random.normal(first, (S, R), jnp.float32)
    factor = column_factor(third, labels, groups)
    return (jnp.exp(2.0 * noise - 2.0) * factor / S).astype(jnp.bfloat16)


def touch_ends(drawn, own_key, least, high):
    longest = drawn.shape.index(max(drawn.shape))
    spots = []
    for shift in (0, 1):
        where = [jax.random.randint(jax.random.fold_in(own_key, axis), (), 0, length) for axis, length in enumerate(drawn.shape)]
        where[longest] = (where[longest] + shift) % drawn.shape[longest]
        spots.append(tuple(where))
    return drawn.at[spots[0]].set(least).at[spots[1]].set(high)


def level_of(own_key, dims, shards, smallest, high):
    def one(position, blocks):
        draws = jax.random.uniform(jax.random.fold_in(jax.random.fold_in(own_key, 6), position), (blocks,), jnp.float32, smallest / len(shards), high / len(shards))
        return jnp.repeat(jnp.exp(draws), dims[position] // blocks).reshape((-1,) + (1,) * (len(dims) - position - 1))

    factor_of = one(*shards[0])
    for cut in shards[1:]:
        factor_of = factor_of * one(*cut)
    return factor_of


def rank_table(amount, skew):
    loads = [(1 << 20) // math.isqrt(grade ** skew) + 1 for grade in range(1, amount + 1)]
    spread = 1 + sum(loads) // (1 << 30)
    return np.cumsum(np.array([max(1, weight // spread) for weight in loads]))


def skewed_ids(own_key, extent, amount, skew):
    listing = rank_table(amount, skew)
    lot = jax.random.randint(jax.random.fold_in(own_key, 1), extent, 0, int(listing[amount - 1]))
    rank = jnp.searchsorted(jnp.asarray(listing, jnp.int32), lot, side="right")
    return jax.random.permutation(jax.random.fold_in(own_key, 2), amount)[rank].astype(jnp.int32)


def normal_values(stream_key, shape, width, limit, kind=jnp.bfloat16):
    entries = width * jax.random.normal(stream_key, shape, jnp.float32)
    return jnp.clip(entries, min=-limit, max=limit).astype(kind)


def setup_inputs(seed: int = 0) -> dict:
    keys = jax.random.split(jax.random.key(seed), 9)
    token_ids = touch_ends(skewed_ids(keys[0], (STEPS, B), VOCAB, 2), jax.random.fold_in(keys[0], 3), 0, VOCAB - 1).astype(jnp.int32)
    word_emb = normal_values(keys[1], (VOCAB, H), 1.0, 6.0)
    state_emb = draw_state_emb(jax.random.fold_in(keys[8], 71), 0)
    log_norm = jnp.clip(-0.5 + 1.5 * jax.random.uniform(keys[3], (S,), jnp.float32) ** level_of(keys[3], (S,), ((0, 8),), -0.2, 0.2), -0.5, 1.0)
    beta_last = jnp.clip(jnp.exp(math.log(5.0) - 3.2227897 * jax.random.uniform(keys[4], (S, B), jnp.float32) ** level_of(keys[4], (S, B), ((0, 8),), -0.2, 0.2)), 0.19921875, 5.0).astype(jnp.bfloat16)
    forward_marg = jnp.clip(jnp.exp(math.log(2.0) - 3.6927934 * jax.random.uniform(keys[5], (S, STEPS * B), jnp.float32) ** level_of(keys[5], (S, STEPS * B), ((0, 8),), -0.2, 0.2)), 0.049804688, 2.0).astype(jnp.bfloat16)
    trans_left = draw_trans_left(jax.random.fold_in(keys[8], 71), 0)
    trans_right = draw_trans_right(jax.random.fold_in(keys[8], 71), 0)
    return {"token_ids": token_ids, "word_emb": word_emb, "state_emb": state_emb, "log_norm": log_norm, "beta_last": beta_last, "forward_marg": forward_marg, "trans_left": trans_left, "trans_right": trans_right}


def reference(token_ids, word_emb, state_emb, log_norm, beta_last, forward_marg, trans_left, trans_right):
    beta = beta_last
    weighted_list = []
    proj_list = []
    for step in reversed(range(STEPS)):
        words = jnp.take(word_emb, token_ids[step], axis=0)
        logits = jnp.dot(state_emb, words.T, preferred_element_type=jnp.float32)
        emit = jnp.exp(logits - log_norm[:, None])
        weighted = (emit * beta.astype(jnp.float32)).astype(jnp.bfloat16)
        proj = lax.dot_general(weighted, trans_right, (((0,), (0,)), ((), ())), preferred_element_type=jnp.float32)
        projb = proj.astype(jnp.bfloat16)
        raw = lax.dot_general(trans_left, projb, (((1,), (1,)), ((), ())), preferred_element_type=jnp.float32)
        mass = jnp.sum(raw, axis=0) / S
        beta = (raw / mass[None, :]).astype(jnp.bfloat16)
        weighted_list.insert(0, weighted)
        proj_list.insert(0, projb)
    weighted_all = jnp.concatenate(weighted_list, axis=1)
    proj_all = jnp.concatenate(proj_list, axis=0)
    fwd_proj = lax.dot_general(forward_marg, trans_left, (((0,), (0,)), ((), ())), preferred_element_type=jnp.float32)
    fwd_proj = (fwd_proj / S).astype(jnp.bfloat16)
    count = STEPS * B
    grad_left = (jnp.dot(forward_marg, proj_all, preferred_element_type=jnp.float32) / count).astype(jnp.bfloat16)
    grad_right = (jnp.dot(weighted_all, fwd_proj, preferred_element_type=jnp.float32) / count).astype(jnp.bfloat16)
    return beta, grad_left, grad_right
```

```python
import jax
import jax.numpy as jnp
from jax import lax
from jax.sharding import PartitionSpec as P


def send_by(value, axis, offset):
    count = lax.axis_size(axis)
    return lax.ppermute(value, axis, [(i, (i + offset) % count) for i in range(count)])


def send_xor(value, axis, bit):
    count = lax.axis_size(axis)
    return lax.ppermute(value, axis, [(i, i ^ bit) for i in range(count)])


def sum_small(value, axis):
    bit = 1
    while bit < lax.axis_size(axis):
        value = value + send_xor(value, axis, bit)
        bit *= 2
    return value


def sum_over_state(part, scale):
    count = lax.axis_size("state")
    me = lax.axis_index("state")
    rows, columns = part.shape
    pieces = part.astype(jnp.bfloat16).reshape(count, rows // count, columns)

    def piece(index):
        return lax.dynamic_index_in_dim(pieces, index % count, 0, keepdims=False)

    total = lax.dynamic_index_in_dim(
        part.reshape(count, rows // count, columns), me, 0, keepdims=False
    )
    for offset in range(1, count):
        got = send_by(piece(me + offset), "state", offset)
        total = total + got.astype(jnp.float32)
    mine = (total * scale).astype(jnp.bfloat16)
    held = [mine] + [send_by(mine, "state", offset) for offset in range(1, count)]
    stacked = jnp.stack(held[::-1])
    ordered = jnp.roll(stacked, me + 1, axis=0)
    return ordered.reshape(rows, columns)


def sum_over_rank(raw_part, mass_part):
    count = lax.axis_size("rank")
    me = lax.axis_index("rank")
    half = raw_part.shape[0] // 2
    low = me % 2
    own = lax.dynamic_slice_in_dim(raw_part, low * half, half, 0)
    other = lax.dynamic_slice_in_dim(raw_part, (1 - low) * half, half, 0)
    total = own + send_xor(other.astype(jnp.bfloat16), "rank", 1).astype(jnp.float32)
    bit = 2
    while bit < count:
        rounded = total.astype(jnp.bfloat16)
        got = send_xor(rounded, "rank", bit)
        total = rounded.astype(jnp.float32) + got.astype(jnp.float32)
        bit *= 2
    mass = sum_small(mass_part, "rank")
    return total, mass


def both_halves(value):
    low = lax.axis_index("rank") % 2
    got = send_xor(value, "rank", 1)
    first = jnp.where(low == 0, value, got)
    second = jnp.where(low == 0, got, value)
    return jnp.concatenate([first, second], axis=0)


def on_device(
    token_ids, word_emb, state_emb, log_norm, beta_last, forward_marg, trans_left, trans_right
):
    states_all = lax.axis_size("state") * state_emb.shape[0]
    steps, batch = token_ids.shape
    column_sums = sum_small(jnp.sum(trans_left, axis=0, dtype=jnp.float32), "state")
    words_all = jnp.take(word_emb, token_ids.reshape(-1), axis=0)
    logits = jnp.dot(state_emb, words_all.T, preferred_element_type=jnp.float32)
    emit_all = jnp.exp(logits - log_norm[:, None])
    beta = beta_last
    weighted_list = []
    proj_list = []
    fwd_proj = None
    for step in reversed(range(steps)):
        emit = emit_all[:, step * batch : (step + 1) * batch]
        weighted = (emit * beta.astype(jnp.float32)).astype(jnp.bfloat16)
        proj_part = lax.dot_general(
            weighted, trans_right, (((0,), (0,)), ((), ())), preferred_element_type=jnp.float32
        )
        projb = sum_over_state(proj_part, 1.0)
        mass_part = jnp.dot(projb.astype(jnp.float32), column_sums)
        raw_part = lax.dot_general(
            trans_left, projb, (((1,), (1,)), ((), ())), preferred_element_type=jnp.float32
        )
        raw_half, total = sum_over_rank(raw_part, mass_part)
        mass = total / states_all
        beta = both_halves((raw_half / mass[None, :]).astype(jnp.bfloat16))
        if fwd_proj is None:
            fwd_part = lax.dot_general(
                forward_marg,
                trans_left,
                (((0,), (0,)), ((), ())),
                preferred_element_type=jnp.float32,
            )
            fwd_proj = sum_over_state(fwd_part, 1.0 / states_all)
        weighted_list.insert(0, weighted)
        proj_list.insert(0, projb)
    weighted_all = jnp.concatenate(weighted_list, axis=1)
    proj_all = jnp.concatenate(proj_list, axis=0)
    count = steps * batch
    grad_left = (
        jnp.dot(forward_marg, proj_all, preferred_element_type=jnp.float32) / count
    ).astype(jnp.bfloat16)
    grad_right = (
        jnp.dot(weighted_all, fwd_proj, preferred_element_type=jnp.float32) / count
    ).astype(jnp.bfloat16)
    return (beta, grad_left, grad_right)


def solution(mesh):
    placed = (
        P(),
        P(),
        P("state", None),
        P("state"),
        P("state", None),
        P("state", None),
        P("state", "rank"),
        P("state", "rank"),
    )
    return jax.shard_map(
        on_device,
        mesh=mesh,
        in_specs=placed,
        out_specs=(P("state", None), P("state", "rank"), P("state", "rank")),
        check_vma=False,
    )
```

```python
import jax
import jax.numpy as jnp
from jax import lax
from jax.sharding import PartitionSpec as P


def send_xor(value, axis, bit):
    count = lax.axis_size(axis)
    return lax.ppermute(value, axis, [(i, i ^ bit) for i in range(count)])


def sum_small(value, axis):
    bit = 1
    while bit < lax.axis_size(axis):
        value = value + send_xor(value, axis, bit)
        bit *= 2
    return value


def sum_over_state(part, scale):
    count = lax.axis_size("state")
    rows, columns = part.shape
    pieces = lax.all_to_all(part.astype(jnp.bfloat16), "state", 0, 0, tiled=True)
    total = jnp.sum(pieces.reshape(count, rows // count, columns), axis=0, dtype=jnp.float32)
    mine = (total * scale).astype(jnp.bfloat16)
    spread = jnp.broadcast_to(mine[None], (count,) + mine.shape).reshape(rows, columns)
    return lax.all_to_all(spread, "state", 0, 0, tiled=True)


def sum_over_rank(raw_part, mass_part):
    count = lax.axis_size("rank")
    me = lax.axis_index("rank")
    half = raw_part.shape[0] // 2
    low = me % 2
    own = lax.dynamic_slice_in_dim(raw_part, low * half, half, 0)
    other = lax.dynamic_slice_in_dim(raw_part, (1 - low) * half, half, 0)
    total = own + send_xor(other.astype(jnp.bfloat16), "rank", 1).astype(jnp.float32)
    bit = 2
    while bit < count:
        rounded = total.astype(jnp.bfloat16)
        got = send_xor(rounded, "rank", bit)
        total = rounded.astype(jnp.float32) + got.astype(jnp.float32)
        bit *= 2
    mass = sum_small(mass_part, "rank")
    return total, mass


def both_halves(value):
    low = lax.axis_index("rank") % 2
    got = send_xor(value, "rank", 1)
    first = jnp.where(low == 0, value, got)
    second = jnp.where(low == 0, got, value)
    return jnp.concatenate([first, second], axis=0)


def on_device(
    token_ids, word_emb, state_emb, log_norm, beta_last, forward_marg, trans_left, trans_right
):
    states_all = lax.axis_size("state") * state_emb.shape[0]
    steps, batch = token_ids.shape
    column_sums = sum_small(jnp.sum(trans_left, axis=0, dtype=jnp.float32), "state")
    words_all = jnp.take(word_emb, token_ids.reshape(-1), axis=0)
    logits = jnp.dot(state_emb, words_all.T, preferred_element_type=jnp.float32)
    emit_all = jnp.exp(logits - log_norm[:, None])
    beta = beta_last
    weighted_list = []
    proj_list = []
    fwd_proj = None
    for step in reversed(range(steps)):
        emit = emit_all[:, step * batch : (step + 1) * batch]
        weighted = (emit * beta.astype(jnp.float32)).astype(jnp.bfloat16)
        proj_part = lax.dot_general(
            weighted, trans_right, (((0,), (0,)), ((), ())), preferred_element_type=jnp.float32
        )
        projb = sum_over_state(proj_part, 1.0)
        mass_part = jnp.dot(projb.astype(jnp.float32), column_sums)
        raw_part = lax.dot_general(
            trans_left, projb, (((1,), (1,)), ((), ())), preferred_element_type=jnp.float32
        )
        raw_half, total = sum_over_rank(raw_part, mass_part)
        mass = total / states_all
        beta = both_halves((raw_half / mass[None, :]).astype(jnp.bfloat16))
        if fwd_proj is None:
            fwd_part = lax.dot_general(
                forward_marg,
                trans_left,
                (((0,), (0,)), ((), ())),
                preferred_element_type=jnp.float32,
            )
            fwd_proj = sum_over_state(fwd_part, 1.0 / states_all)
        weighted_list.insert(0, weighted)
        proj_list.insert(0, projb)
    weighted_all = jnp.concatenate(weighted_list, axis=1)
    proj_all = jnp.concatenate(proj_list, axis=0)
    count = steps * batch
    grad_left = (
        jnp.dot(forward_marg, proj_all, preferred_element_type=jnp.float32) / count
    ).astype(jnp.bfloat16)
    grad_right = (
        jnp.dot(weighted_all, fwd_proj, preferred_element_type=jnp.float32) / count
    ).astype(jnp.bfloat16)
    return (beta, grad_left, grad_right)


def solution(mesh):
    placed = (
        P(),
        P(),
        P("state", None),
        P("state"),
        P("state", None),
        P("state", None),
        P("state", "rank"),
        P("state", "rank"),
    )
    return jax.shard_map(
        on_device,
        mesh=mesh,
        in_specs=placed,
        out_specs=(P("state", None), P("state", "rank"), P("state", "rank")),
        check_vma=False,
    )
```

```python
import functools

import jax
import jax.numpy as jnp
from jax import lax
from jax.experimental import pallas as pl
from jax.experimental.pallas import tpu as pltpu
from jax.sharding import PartitionSpec as P

F32 = jnp.float32
BF16 = jnp.bfloat16


def swap(value, axis, bit):
    count = lax.axis_size(axis)
    return lax.ppermute(value, axis, [(i, i ^ bit) for i in range(count)])


def dot_nt(a, b):
    return lax.dot_general(a, b, (((1,), (1,)), ((), ())), preferred_element_type=F32)


def dot_tn(a, b):
    return lax.dot_general(a, b, (((0,), (0,)), ((), ())), preferred_element_type=F32)


def first_kernel(words, emb, norm, beta, right, weighted, proj):
    emit = jnp.exp(dot_nt(words[...], emb[...]) - norm[...])
    value = (emit * beta[...].astype(F32).T).astype(BF16)
    weighted[...] = value

    @pl.when(pl.program_id(0) == 0)
    def _():
        proj[...] = jnp.zeros_like(proj)

    proj[...] += jnp.dot(value, right[...], preferred_element_type=F32)


def first_weighted(words, emb, norm, beta, right, tile):
    states, width = emb.shape
    batch = words.shape[0]
    columns = right.shape[1]
    return pl.pallas_call(
        first_kernel,
        grid=(states // tile,),
        in_specs=[
            pl.BlockSpec((batch, width), lambda i: (0, 0)),
            pl.BlockSpec((tile, width), lambda i: (i, 0)),
            pl.BlockSpec((1, tile), lambda i: (0, i)),
            pl.BlockSpec((tile, batch), lambda i: (i, 0)),
            pl.BlockSpec((tile, columns), lambda i: (i, 0)),
        ],
        out_specs=[
            pl.BlockSpec((batch, tile), lambda i: (0, i)),
            pl.BlockSpec((batch, columns), lambda i: (0, 0)),
        ],
        out_shape=[
            jax.ShapeDtypeStruct((batch, states), BF16),
            jax.ShapeDtypeStruct((batch, columns), F32),
        ],
        cost_estimate=pl.CostEstimate(
            flops=2 * states * batch * (columns + width),
            bytes_accessed=2 * states * (columns + width + 2 * batch),
            transcendentals=states * batch,
        ),
        name="first_weighted",
    )(words, emb, norm, beta, right)


def prepare_kernel(left, words, emb, norm, flipped, sums, emit):
    block = left[...]
    flipped[...] = block.T
    emit[...] = jnp.exp(dot_nt(words[...], emb[...]) - norm[...])

    @pl.when(pl.program_id(0) == 0)
    def _():
        sums[...] = jnp.zeros_like(sums)

    sums[...] += jnp.broadcast_to(
        jnp.sum(block.astype(F32), axis=0, keepdims=True), sums.shape
    )


def prepare(left, words, emb, norm, tile):
    states, columns = left.shape
    rows, width = words.shape
    return pl.pallas_call(
        prepare_kernel,
        grid=(states // tile,),
        in_specs=[
            pl.BlockSpec((tile, columns), lambda i: (i, 0)),
            pl.BlockSpec((rows, width), lambda i: (0, 0)),
            pl.BlockSpec((tile, width), lambda i: (i, 0)),
            pl.BlockSpec((1, tile), lambda i: (0, i)),
        ],
        out_specs=[
            pl.BlockSpec((columns, tile), lambda i: (0, i)),
            pl.BlockSpec((16, columns), lambda i: (0, 0)),
            pl.BlockSpec((rows, tile), lambda i: (0, i)),
        ],
        out_shape=[
            jax.ShapeDtypeStruct((columns, states), BF16),
            jax.ShapeDtypeStruct((16, columns), F32),
            jax.ShapeDtypeStruct((rows, states), F32),
        ],
        cost_estimate=pl.CostEstimate(
            flops=2 * states * rows * width,
            bytes_accessed=states * (4 * columns + 4 * rows + 2 * width),
            transcendentals=states * rows,
        ),
        name="prepare",
    )(left, words, emb, norm)


def grads_kernel(scale, marg, proj, fwd, *refs):
    weighted, (grad_left, grad_right) = refs[:-2], refs[-2:]
    grad_left[...] = (
        jnp.dot(marg[...], proj[...], preferred_element_type=F32) * scale
    ).astype(BF16)
    rows = jnp.concatenate([ref[...] for ref in weighted], axis=0)
    grad_right[...] = (dot_tn(rows, fwd[...]) * scale).astype(BF16)


def gradients(marg, proj, fwd, weighted, tile):
    states, rows = marg.shape
    columns = proj.shape[1]
    return pl.pallas_call(
        functools.partial(grads_kernel, 1.0 / rows),
        grid=(states // tile,),
        in_specs=[
            pl.BlockSpec((tile, rows), lambda i: (i, 0)),
            pl.BlockSpec((rows, columns), lambda i: (0, 0)),
            pl.BlockSpec((rows, columns), lambda i: (0, 0)),
        ]
        + [pl.BlockSpec((w.shape[0], tile), lambda i: (0, i)) for w in weighted],
        out_specs=[pl.BlockSpec((tile, columns), lambda i: (i, 0))] * 2,
        out_shape=[jax.ShapeDtypeStruct((states, columns), BF16)] * 2,
        cost_estimate=pl.CostEstimate(
            flops=4 * states * rows * columns,
            bytes_accessed=4 * states * (rows + columns),
            transcendentals=0,
        ),
        name="gradients",
    )(marg, proj, fwd, *weighted)


def flip_kernel(first, second, out):
    out[...] = jnp.concatenate([first[...], second[...]], axis=0).astype(F32).T.astype(BF16)


def flip(first, second, tile):
    half, states = first.shape
    return pl.pallas_call(
        flip_kernel,
        grid=(states // tile,),
        in_specs=[pl.BlockSpec((half, tile), lambda i: (0, i))] * 2,
        out_specs=pl.BlockSpec((tile, 2 * half), lambda i: (i, 0)),
        out_shape=jax.ShapeDtypeStruct((states, 2 * half), BF16),
        name="flip",
    )(first, second)


def sum_over_state(keep, sent, extra=None):
    half = keep.shape[0]
    total = keep + swap(sent.astype(BF16), "state", 1).astype(F32)
    if extra is not None:
        total = jnp.concatenate([total, extra], axis=0)
    bit = 2
    while bit < lax.axis_size("state"):
        total = total + swap(total.astype(BF16), "state", bit).astype(F32)
        bit *= 2
    mine = total[:half].astype(BF16)
    if extra is None:
        return mine, swap(mine, "state", 1), None
    extra = total[half:]
    got = swap(jnp.concatenate([mine, extra.astype(BF16)], axis=0), "state", 1)
    return mine, got[:half], extra + got[half:].astype(F32)


def on_device(
    token_ids, word_emb, state_emb, log_norm, beta_last, forward_marg, trans_left, trans_right
):
    steps, batch = token_ids.shape
    half = batch // 2
    states = state_emb.shape[0]
    states_all = lax.axis_size("state") * states
    tile = 512
    low = lax.axis_index("rank") % 2
    side = lax.axis_index("state") % 2
    same = low == side

    words = word_emb.at[token_ids.reshape(-1)].get(mode="promise_in_bounds")
    norm = log_norm.reshape(1, states)
    last = (steps - 1) * batch
    weighted, proj_part = first_weighted(
        words[last:], state_emb, norm, beta_last, trans_right, tile
    )
    flipped, column_sums, emit_all = prepare(trans_left, words[:last], state_emb, norm, tile)

    def take_half(value, which):
        return lax.dynamic_slice_in_dim(value, which * half, half, 0)

    keep, sent = take_half(proj_part, side), take_half(proj_part, 1 - side)
    pieces = {steps - 1: [weighted[:half], weighted[half:]]}
    order = {steps - 1: [0, 1]}
    proj_rows = {}
    fwd = None
    beta = None
    for step in reversed(range(steps)):
        if step == steps - 1:
            mine, got, sums = sum_over_state(keep, sent, column_sums)
            column_sums = sums[:1]
        else:
            mine, got, _ = sum_over_state(keep, sent)
        proj_own = jnp.where(same, mine, got)
        proj_mate = jnp.where(same, got, mine)
        proj_rows[step] = [
            jnp.where(side == 0, mine, got),
            jnp.where(side == 0, got, mine),
        ]
        mass = jnp.sum(proj_own.astype(F32) * column_sums, axis=1)
        mass_mate = jnp.sum(proj_mate.astype(F32) * column_sums, axis=1)
        mass = mass + swap(mass_mate, "rank", 1)
        bit = 2
        while bit < lax.axis_size("rank"):
            mass = mass + swap(mass, "rank", bit)
            bit *= 2
        raw_mate = jnp.dot(proj_mate, flipped, preferred_element_type=F32).astype(BF16)
        raw_got = swap(raw_mate, "rank", 1)
        raw_own = jnp.dot(proj_own, flipped, preferred_element_type=F32)
        raw = raw_own + raw_got.astype(F32)
        bit = 2
        while bit < lax.axis_size("rank"):
            raw, mass = lax.optimization_barrier((raw, mass))
            raw = lax.reduce_precision(raw, 8, 7)
            raw = raw + swap(raw.astype(BF16), "rank", bit).astype(F32)
            bit *= 2
        scaled = raw * (states_all / mass)[:, None]
        if fwd is None:
            fwd_part = dot_tn(forward_marg, trans_left)
            rows = fwd_part.shape[0] // 2
            fwd_mine, fwd_got, _ = sum_over_state(
                lax.dynamic_slice_in_dim(fwd_part, side * rows, rows, 0) / states_all,
                lax.dynamic_slice_in_dim(fwd_part, (1 - side) * rows, rows, 0) / states_all,
            )
            fwd = jnp.concatenate(
                [
                    jnp.where(side == 0, fwd_mine, fwd_got),
                    jnp.where(side == 0, fwd_got, fwd_mine),
                ],
                axis=0,
            )
        if step == 0:
            beta_own = scaled.astype(BF16)
            beta_mate = swap(beta_own, "rank", 1)
            first = jnp.where(low == 0, beta_own, beta_mate)
            second = jnp.where(low == 0, beta_mate, beta_own)
            beta = flip(first, second, tile)
            break
        emit = lax.dynamic_slice_in_dim(
            emit_all, (step - 1) * batch + low * half, half, 0
        )
        own = (emit * scaled).astype(BF16)
        mate = swap(own, "rank", 1)
        part_own = jnp.dot(own, trans_right, preferred_element_type=F32)
        part_mate = jnp.dot(mate, trans_right, preferred_element_type=F32)
        keep = jnp.where(same, part_own, part_mate)
        sent = jnp.where(same, part_mate, part_own)
        pieces[step - 1] = [own, mate]
        order[step - 1] = [low, 1 - low]

    proj_all = jnp.concatenate([p for step in range(steps) for p in proj_rows[step]], axis=0)
    weighted_list, fwd_list = [], []
    for step in range(steps):
        for piece, place in zip(pieces[step], order[step]):
            weighted_list.append(piece)
            fwd_list.append(
                lax.dynamic_slice_in_dim(fwd, step * batch + place * half, half, 0)
            )
    grad_left, grad_right = gradients(
        forward_marg, proj_all, jnp.concatenate(fwd_list, axis=0), weighted_list, tile
    )
    return (beta, grad_left, grad_right)


def solution(mesh):
    placed = (
        P(),
        P(),
        P("state", None),
        P("state"),
        P("state", None),
        P("state", None),
        P("state", "rank"),
        P("state", "rank"),
    )
    return jax.shard_map(
        on_device,
        mesh=mesh,
        in_specs=placed,
        out_specs=(P("state", None), P("state", "rank"), P("state", "rank")),
        check_vma=False,
    )
```
